32 devices in a mesh: ctx: 16 (over z, y, core), head: 2 (over x).
Axes of the slice: x: 2, y: 2, z: 4, core: 2. Of those that a mesh axis runs over, the one named last changes fastest.
Arguments:
- queries: bfloat16 [2048, 16, 128], P('ctx', 'head'), may hold values from -30 to 30
- rotated_keys: bfloat16 [2048, 8, 128], P('ctx', 'head'), may hold values from -4 to 4
- value_vectors: bfloat16 [2048, 8, 128], P('ctx', 'head'), may hold values from -6 to 6
- out_grad: bfloat16 [2048, 5376], P('ctx', 'head'), may hold values from -6 to 6
- out_proj: bfloat16 [5376, 2048], P('ctx', 'head'), may hold values from -0.125 to 0.125
- seg_ids: int32 [2048], replicated, may hold values from 0 to 3, never falling along the last dimension, each value on 1 to 1024 neighbouring positions
Outputs:
- layer_out: bfloat16 [2048, 5376], P('ctx', 'head')
- query_gradient: bfloat16 [2048, 16, 128], P('ctx', 'head')
- grad_key: bfloat16 [2048, 8, 128], P('ctx', 'head')
- grad_value: bfloat16 [2048, 8, 128], P('ctx', 'head')
- grad_proj: float32 [5376, 2048], P('ctx', 'head')
The draws below stay inside these ranges and needn't reach their ends.
Inputs may be any that keep to these rules, and one draw needn't show every extreme that they name: `seg_ids`: segment ids never fall along the slab; every one of the 4 books holds one token or more.
All inputs are finite; a program needn't handle non-finite values.
Results may differ from the reference program's by a relative error of at most 0.025.
Values may be sent and summed in bfloat16 or wider, within the bound.
A program may use at most 128 MiB of HBM per device.

```python
import math
import jax
import jax.numpy as jnp
import numpy as np
from jax import lax

D = 5376
HEAD_WIDTH = 128
WINDOW_TOKENS = 1024
HQ = 16
KEY_VALUE_HEADS = 8
SLAB_TOKENS = 2048
QUERIES_PER_KV = 2
SEGMENTS = 4


def drawn_pair(key):
    base_key = jax.random.fold_in(key, 4711)
    first_key, second_random_key = jax.random.split(base_key, 2)
    query_draw = jnp.clip(2.5 * jax.random.normal(first_key, (SLAB_TOKENS, HQ, HEAD_WIDTH), jnp.float32), -10.0, 10.0)
    random_key_draw = jnp.clip(jax.random.normal(second_random_key, (SLAB_TOKENS, KEY_VALUE_HEADS, HEAD_WIDTH), jnp.float32), -4.0, 4.0)
    return (query_draw, random_key_draw)


def draw_queries(key, part):
    return drawn_pair(key)[0].astype(jnp.bfloat16)


def draw_rotated_keys(key, part):
    return drawn_pair(key)[1].astype(jnp.bfloat16)


def with_spikes(result, own_key, source, target, parts, factor):
    owner, partner = [(jnp.arange(result.shape[position]) // (result.shape[position] // parts)).reshape([-1 if axis == position else 1 for axis in range(result.ndim)]) for position in (source, target)]
    chosen = jax.random.permutation(own_key, parts)[partner]
    strong = (owner == chosen) | (owner == (partner + parts // 2) % parts)
    return jnp.where(strong, factor * result, result)


def block_scale(rng, dims, cuts, low, top_value):
    level = 1.0
    for position, shards_of in cuts:
        steps = jax.random.uniform(jax.random.fold_in(jax.random.fold_in(rng, 6), position), (shards_of,), jnp.float32, low / len(cuts), top_value / len(cuts))
        level = level * jnp.repeat(jnp.exp(steps), dims[position] // shards_of).reshape((-1,) + (1,) * (len(dims) - 1 - position))
    return level


def profile(count, total, bound, skew):
    loads = [(1 << 20) // math.isqrt(grade ** skew) + 1 for grade in range(2, count + 1)]
    spare, counts = total - bound - (count - 1), [1] * (count - 1)
    while spare > 0:
        movable = [i for i in range(count - 1) if counts[i] < bound]
        mass, left = sum([loads[i] for i in movable]), spare
        for i in movable:
            more = min(bound - counts[i], max(1, left * loads[i] // mass), spare)
            counts[i] = counts[i] + more
            spare = spare - more
    return np.array([bound] + counts)


def uneven_parts(rng, amount, total, reach, skew):
    if amount == 2:
        one = jax.random.randint(rng, (), max(1, total - reach), min(reach, total - 1) + 1)
        return jnp.stack([one, total - one])
    lengths = jnp.asarray(profile(amount, total, reach, skew), jnp.int32)
    twos = (amount - 1) // 2
    source_of, taker = lengths[1:1 + 2 * twos:2], lengths[2:2 + 2 * twos:2]
    slack = jnp.minimum(source_of - 1, reach - taker)
    moved = jax.random.randint(jax.random.fold_in(rng, 1), (twos,), 0, 1 << 20) % (slack + 1)
    lengths = lengths.at[1:1 + 2 * twos:2].set(source_of - moved).at[2:2 + 2 * twos:2].set(taker + moved)
    return lengths[jax.random.permutation(jax.random.fold_in(rng, 2), amount)]


def normal_values(key, extent, scale, most, pieces=(), kind=jnp.bfloat16):
    values = jax.random.normal(key, extent, jnp.float32) * scale
    if len(pieces) > 0:
        values = block_scale(key, extent, pieces, -0.22, 0.18) * values
    return jnp.clip(values, min=-most, max=most).astype(kind)


def bell_draw_with(rng, shape, spread, reach, cuts, heavy, kind=jnp.bfloat16):
    result = spread * jax.random.normal(rng, shape, jnp.float32)
    if cuts:
        result = result * block_scale(rng, shape, cuts, -0.22, 0.18)
    return jnp.clip(with_spikes(result, jax.random.fold_in(rng, 3), *heavy), -reach, reach).astype(kind)


def setup_inputs(seed: int = 0) -> dict:
    seeds = jax.random.split(jax.random.key(seed), 7)
    return {
        "queries": draw_queries(jax.random.fold_in(seeds[6], 71), 0),
        "rotated_keys": draw_rotated_keys(jax.random.fold_in(seeds[6], 71), 0),
        "value_vectors": normal_values(seeds[2], (SLAB_TOKENS, KEY_VALUE_HEADS, HEAD_WIDTH), 1.0, 6.0, ((0, 16), (1, 2))),
        "out_grad": bell_draw_with(seeds[3], (SLAB_TOKENS, D), 1.0, 6.0, ((0, 16), (1, 2)), (0, 1, 16, 2.0)),
        "out_proj": normal_values(seeds[4], (D, HQ * HEAD_WIDTH), (HQ * HEAD_WIDTH) ** -0.5, 0.125, ((0, 16), (1, 2))),
        "seg_ids": jnp.searchsorted(jnp.cumsum(uneven_parts(seeds[5], SEGMENTS, SLAB_TOKENS, SLAB_TOKENS // 2, 2)), jnp.arange(SLAB_TOKENS), side="right").astype(jnp.int32),
    }


def reference(queries, rotated_keys, value_vectors, out_grad, out_proj, seg_ids):
    logit_scale = 168.0 ** -0.5
    rows_per_block = math.gcd(SLAB_TOKENS, 512)
    block_count = SLAB_TOKENS // rows_per_block
    span_rows = WINDOW_TOKENS + rows_per_block
    padded_keys = jnp.concatenate([jnp.zeros((WINDOW_TOKENS, KEY_VALUE_HEADS, HEAD_WIDTH), rotated_keys.dtype), rotated_keys], 0)
    padded_values = jnp.concatenate([jnp.zeros((WINDOW_TOKENS, KEY_VALUE_HEADS, HEAD_WIDTH), value_vectors.dtype), value_vectors], 0)
    seg_whole = seg_ids.astype(jnp.int32)
    seg_padded = jnp.concatenate([jnp.full((WINDOW_TOKENS,), -1, jnp.int32), seg_whole], 0)

    def block_probs(block_index):
        first_row = (block_index * rows_per_block).astype(jnp.int32)
        block_queries = lax.dynamic_slice_in_dim(queries, first_row, rows_per_block, 0).astype(jnp.float32)
        block_queries = block_queries.reshape(rows_per_block, KEY_VALUE_HEADS, QUERIES_PER_KV, HEAD_WIDTH)
        block_keys = lax.dynamic_slice_in_dim(padded_keys, first_row, span_rows, 0).astype(jnp.float32)
        block_values = lax.dynamic_slice_in_dim(padded_values, first_row, span_rows, 0).astype(jnp.float32)
        query_pos = first_row + jnp.arange(rows_per_block, dtype=jnp.int32)
        key_pos = first_row - WINDOW_TOKENS + jnp.arange(span_rows, dtype=jnp.int32)
        query_seg = lax.dynamic_slice_in_dim(seg_whole, first_row, rows_per_block, 0)
        key_seg = lax.dynamic_slice_in_dim(seg_padded, first_row, span_rows, 0)
        allowed = (key_pos[None, :] <= query_pos[:, None]) & (query_pos[:, None] - key_pos[None, :] < WINDOW_TOKENS)
        allowed = allowed & (key_pos[None, :] >= 0) & (query_seg[:, None] == key_seg[None, :])
        attention_logits = jnp.einsum("eqco,fqo->qcef", block_queries, block_keys) * logit_scale
        attention_logits = jnp.where(allowed, attention_logits, -1e30)
        top_score = jnp.max(attention_logits, axis=3, keepdims=True)
        weights = jnp.where(allowed, jnp.exp(attention_logits - top_score), 0.0)
        probs = weights / jnp.sum(weights, axis=3, keepdims=True)
        return probs, block_queries, block_keys, block_values, first_row

    def forward_block(block_index):
        probs, block_queries, block_keys, block_values, first_row = block_probs(block_index)
        rounded_values = probs.astype(jnp.bfloat16).astype(jnp.float32)
        attended_output = jnp.einsum("ykip,pyj->iykj", rounded_values, block_values)
        return attended_output.astype(jnp.bfloat16).reshape(rows_per_block, HQ * HEAD_WIDTH)

    attended_output = lax.map(forward_block, jnp.arange(block_count, dtype=jnp.int32)).reshape(SLAB_TOKENS, HQ * HEAD_WIDTH)
    layer_out = jnp.dot(attended_output, out_proj.T, preferred_element_type=jnp.float32).astype(jnp.bfloat16)
    grad_attended = jnp.dot(out_grad, out_proj, preferred_element_type=jnp.float32).astype(jnp.bfloat16)
    grad_proj = jnp.dot(out_grad.T, attended_output, preferred_element_type=jnp.float32) * (SLAB_TOKENS ** -0.5)

    def backward_block(carry, block_index):
        key_sum, value_sum = carry
        probs, block_queries, block_keys, block_values, first_row = block_probs(block_index)
        rounded_values = probs.astype(jnp.bfloat16).astype(jnp.float32)
        block_gradient = lax.dynamic_slice_in_dim(grad_attended, first_row, rows_per_block, 0).astype(jnp.float32)
        block_gradient = block_gradient.reshape(rows_per_block, KEY_VALUE_HEADS, QUERIES_PER_KV, HEAD_WIDTH)
        attention_block = lax.dynamic_slice_in_dim(attended_output, first_row, rows_per_block, 0).astype(jnp.float32)
        attention_block = attention_block.reshape(rows_per_block, KEY_VALUE_HEADS, QUERIES_PER_KV, HEAD_WIDTH)
        probability_gradient = jnp.einsum("eqco,fqo->qcef", block_gradient, block_values)
        row_delta = jnp.transpose(jnp.sum(block_gradient * attention_block, axis=3), (1, 2, 0))[..., None]
        score_gradient = (probs * (probability_gradient - row_delta)).astype(jnp.bfloat16).astype(jnp.float32)
        query_gradient = logit_scale * jnp.einsum("ykip,pyj->iykj", score_gradient, block_keys)
        query_gradient = query_gradient.astype(jnp.bfloat16).reshape(rows_per_block, HQ, HEAD_WIDTH)
        key_portion = logit_scale * jnp.einsum("huoe,ohul->ehl", score_gradient, block_queries)
        value_portion = jnp.einsum("huoe,ohul->ehl", rounded_values, block_gradient)
        key_sum = lax.dynamic_update_slice_in_dim(
            key_sum, lax.dynamic_slice_in_dim(key_sum, first_row, span_rows, 0) + key_portion, first_row, 0)
        value_sum = lax.dynamic_update_slice_in_dim(
            value_sum, lax.dynamic_slice_in_dim(value_sum, first_row, span_rows, 0) + value_portion, first_row, 0)
        return (key_sum, value_sum), query_gradient

    zero_sum_rows = jnp.zeros((SLAB_TOKENS + WINDOW_TOKENS, KEY_VALUE_HEADS, HEAD_WIDTH), jnp.float32)
    (key_sum, value_sum), query_gradient = lax.scan(
        backward_block, (zero_sum_rows, zero_sum_rows), jnp.arange(block_count, dtype=jnp.int32))
    query_gradient = query_gradient.reshape(SLAB_TOKENS, HQ, HEAD_WIDTH)
    grad_key = key_sum[WINDOW_TOKENS:].astype(jnp.bfloat16)
    grad_value = value_sum[WINDOW_TOKENS:].astype(jnp.bfloat16)
    return (layer_out, query_gradient, grad_key, grad_value, grad_proj)
```

```python
import jax
import jax.numpy as jnp
from jax import lax
from jax.sharding import PartitionSpec as P

WINDOW_TOKENS = 1024
BF16 = jnp.bfloat16
F32 = jnp.float32


def shifted(value, axis, by):
    count = lax.axis_size(axis)
    pairs = [(i, i + by) for i in range(count) if 0 <= i + by < count]
    return lax.ppermute(value, axis, pairs)


def rotated(value, axis, by):
    count = lax.axis_size(axis)
    return lax.ppermute(value, axis, [(i, (i + by) % count) for i in range(count)])


def matmul(a, b, dims):
    return lax.dot_general(a, b, (dims, ((), ())), preferred_element_type=F32)


def shards(queries, rotated_keys, value_vectors, out_grad, out_proj, seg_ids):
    logit_scale = 168.0 ** (-0.5)
    tok_rows, heads_query, head_size = queries.shape
    heads_kv = rotated_keys.shape[1]
    per_kv = heads_query // heads_kv
    ctx_count = lax.axis_size("ctx")
    head_count = lax.axis_size("head")
    ctx_index = lax.axis_index("ctx")
    head_index = lax.axis_index("head")
    group = heads_kv
    groups = [[g * group + i for i in range(group)] for g in range(ctx_count // group)]
    rows = group * tok_rows
    halo_blocks = WINDOW_TOKENS // rows
    q_width = per_kv * head_size

    def to_heads(value):
        return lax.all_to_all(value, "ctx", 1, 0, axis_index_groups=groups, tiled=True)

    def to_tokens(value):
        return lax.all_to_all(value, "ctx", 0, 1, axis_index_groups=groups, tiled=True)

    packed = jnp.concatenate(
        [queries.reshape(tok_rows, heads_kv, q_width), rotated_keys, value_vectors], axis=2
    )
    mine = to_heads(packed).reshape(rows, q_width + 2 * head_size)
    q = mine[:, :q_width].reshape(rows, per_kv, head_size).transpose(1, 0, 2)
    own_kv = mine[:, q_width:]
    received = [shifted(own_kv, "ctx", group * (d + 1)) for d in range(halo_blocks)]
    kv = jnp.concatenate(received[::-1] + [own_kv], axis=0)
    keys, values = kv[:, :head_size], kv[:, head_size:]

    proj_full = lax.all_gather(out_proj, "ctx", axis=0, tiled=True)

    columns = out_grad.shape[1]
    grad_full = jnp.zeros((tok_rows, columns * head_count), BF16)
    grad_full = lax.dynamic_update_slice_in_dim(grad_full, out_grad, head_index * columns, 1)
    for d in range(1, head_count):
        block = rotated(out_grad, "head", d)
        source = lax.rem(head_index + head_count - d, head_count)
        grad_full = lax.dynamic_update_slice_in_dim(grad_full, block, source * columns, 1)
    grad_columns = lax.all_to_all(grad_full, "ctx", 1, 0, tiled=True)

    first_row = (ctx_index // group) * rows
    seg_padded = jnp.concatenate([jnp.full((WINDOW_TOKENS,), -1, jnp.int32), seg_ids], 0)
    key_seg = lax.dynamic_slice_in_dim(seg_padded, first_row, WINDOW_TOKENS + rows, 0)
    query_seg = lax.dynamic_slice_in_dim(seg_ids, first_row, rows, 0)
    query_pos = first_row + jnp.arange(rows, dtype=jnp.int32)
    key_pos = first_row - WINDOW_TOKENS + jnp.arange(WINDOW_TOKENS + rows, dtype=jnp.int32)
    allowed = (key_pos[None, :] <= query_pos[:, None]) & (
        query_pos[:, None] - key_pos[None, :] < WINDOW_TOKENS
    )
    allowed = allowed & (key_pos[None, :] >= 0) & (query_seg[:, None] == key_seg[None, :])

    scores = logit_scale * jnp.einsum("htd,sd->hts", q, keys, preferred_element_type=F32)
    scores = jnp.where(allowed, scores, -1e30)
    top_score = jnp.max(scores, axis=2, keepdims=True)
    weights = jnp.where(allowed, jnp.exp(scores - top_score), 0.0)
    probs = weights / jnp.sum(weights, axis=2, keepdims=True)
    probs_bf = probs.astype(BF16)
    attended = jnp.einsum("hts,sd->htd", probs_bf, values, preferred_element_type=F32).astype(BF16)
    attended_tok = to_tokens(attended.transpose(1, 0, 2).reshape(rows, q_width))
    attended_all = lax.all_gather(attended_tok, "ctx", axis=0, tiled=True)

    grad_att_tok = matmul(grad_full, proj_full, ((1,), (0,))).astype(BF16)
    grad_att = to_heads(grad_att_tok).reshape(rows, per_kv, head_size).transpose(1, 0, 2)

    def out_columns(which):
        block = lax.dynamic_slice_in_dim(proj_full, which * columns, columns, 0)
        return matmul(attended_tok, block, ((1,), (1,)))

    layer_out = out_columns(head_index)
    for d in range(1, head_count):
        target = lax.rem(head_index + d, head_count)
        layer_out = layer_out + rotated(out_columns(target).astype(BF16), "head", d).astype(F32)
    layer_out = layer_out.astype(BF16)

    grad_proj = matmul(grad_columns, attended_all, ((0,), (0,))) * (ctx_count * tok_rows) ** (-0.5)

    grad_probs = jnp.einsum("htd,sd->hts", grad_att, values, preferred_element_type=F32)
    row_delta = jnp.sum(grad_att.astype(F32) * attended.astype(F32), axis=2, keepdims=True)
    grad_scores = (probs * (grad_probs - row_delta)).astype(BF16)
    grad_k = logit_scale * jnp.einsum("hts,htd->sd", grad_scores, q, preferred_element_type=F32)
    grad_v = jnp.einsum("hts,htd->sd", probs_bf, grad_att, preferred_element_type=F32)
    grad_kv = jnp.concatenate([grad_k, grad_v], axis=1)
    own_grad = grad_kv[WINDOW_TOKENS:]
    for d in range(1, halo_blocks + 1):
        start = WINDOW_TOKENS - d * rows
        own_grad = own_grad + shifted(
            grad_kv[start : start + rows].astype(BF16), "ctx", -group * d
        ).astype(F32)
    grad_q = logit_scale * jnp.einsum("hts,sd->thd", grad_scores, keys, preferred_element_type=F32)
    grads = jnp.concatenate([grad_q.astype(BF16).reshape(rows, q_width), own_grad.astype(BF16)], 1)
    grads = to_tokens(grads).reshape(tok_rows, heads_kv, q_width + 2 * head_size)
    query_gradient = grads[:, :, :q_width].reshape(tok_rows, heads_query, head_size)
    grad_key = grads[:, :, q_width : q_width + head_size]
    grad_value = grads[:, :, q_width + head_size :]
    return (layer_out, query_gradient, grad_key, grad_value, grad_proj)


def solution(mesh):
    tokens_heads = P("ctx", "head", None)
    both = P("ctx", "head")
    return jax.shard_map(
        shards,
        mesh=mesh,
        in_specs=(tokens_heads, tokens_heads, tokens_heads, both, both, P()),
        out_specs=(both, tokens_heads, tokens_heads, tokens_heads, both),
        check_vma=False,
    )
```

```python
import functools

import jax
import jax.numpy as jnp
from jax import lax
from jax.experimental import pallas as pl
from jax.experimental.pallas import tpu as pltpu
from jax.sharding import PartitionSpec as P

WINDOW_TOKENS = 1024
BF16 = jnp.bfloat16
F32 = jnp.float32


def shifted(value, axis, by):
    count = lax.axis_size(axis)
    pairs = [(i, i + by) for i in range(count) if 0 <= i + by < count]
    return lax.ppermute(value, axis, pairs)


def rotated(value, axis, by):
    count = lax.axis_size(axis)
    return lax.ppermute(value, axis, [(i, (i + by) % count) for i in range(count)])


def matmul(a, b, dims):
    return lax.dot_general(a, b, (dims, ((), ())), preferred_element_type=F32)


def ring_place(position, count):
    half = count // 2
    down = position // half
    step = lax.rem(position, half)
    pair, core = step // 2, lax.rem(step, 2)
    level = pair + down * (half // 2 - 1 - 2 * pair)
    return level * 4 + down * 2 + core


def ring_position(index, count):
    half = count // 2
    level, down, core = index // 4, lax.rem(index // 2, 2), lax.rem(index, 2)
    pair = level + down * (half // 2 - 1 - 2 * level)
    return down * half + pair * 2 + core


def ring_kernel(
    count,
    grad_ref,
    proj_ref,
    att_ref,
    all_ref,
    sum_ref,
    out_right,
    out_left,
    in_right,
    in_left,
    gr_send,
    gr_recv,
    gl_send,
    gl_recv,
    sr_send,
    sr_recv,
    sl_send,
    sl_recv,
):
    me = lax.axis_index("ctx")
    here = ring_position(me, count)
    hops_right = count // 2
    hops_left = count - 1 - hops_right

    def place(offset):
        return ring_place(lax.rem(here + offset + count, count), count)

    right, left = {"ctx": place(1)}, {"ctx": place(-1)}
    barrier = pltpu.get_barrier_semaphore()
    for neighbour in (left, right):
        pl.semaphore_signal(
            barrier, inc=1, device_id=neighbour, device_id_type=pl.DeviceIdType.MESH
        )
    pl.semaphore_wait(barrier, 2)

    def remote(src, dst, send, recv, target):
        return pltpu.make_async_remote_copy(
            src_ref=src,
            dst_ref=dst,
            send_sem=send,
            recv_sem=recv,
            device_id=target,
            device_id_type=pl.DeviceIdType.MESH,
        )

    def gather_right(s):
        slot = all_ref.at[place(-s)]
        return remote(slot, slot, gr_send.at[s], gr_recv.at[s], right)

    def gather_left(s):
        slot = all_ref.at[place(s)]
        return remote(slot, slot, gl_send.at[s], gl_recv.at[s], left)

    def sum_right(s):
        return remote(out_right.at[s], in_right.at[s], sr_send.at[s], sr_recv.at[s], right)

    def sum_left(s):
        return remote(out_left.at[s], in_left.at[s], sl_send.at[s], sl_recv.at[s], left)

    def arrived_right(s):
        slot = all_ref.at[place(-s - 1)]
        return remote(slot, slot, gr_send.at[s], gr_recv.at[s], right)

    def arrived_left(s):
        slot = all_ref.at[place(s + 1)]
        return remote(slot, slot, gl_send.at[s], gl_recv.at[s], left)

    def term(offset):
        return jnp.dot(grad_ref[place(offset)], proj_ref[...], preferred_element_type=F32)

    all_ref[me] = att_ref[...]

    def step(s, first, both):
        own = term(hops_right - s)
        if not first:
            sum_right(s - 1).wait_recv()
            own = own + in_right[s - 1].astype(F32)
        out_right[s] = own.astype(BF16)
        sum_right(s).start()
        if both:
            own = term(s - hops_left)
            if not first:
                sum_left(s - 1).wait_recv()
                own = own + in_left[s - 1].astype(F32)
            out_left[s] = own.astype(BF16)
            sum_left(s).start()
        if not first:
            arrived_right(s - 1).wait_recv()
        gather_right(s).start()
        if both:
            if not first:
                arrived_left(s - 1).wait_recv()
            gather_left(s).start()

    def middle(s, carry):
        step(s, False, True)
        return carry

    step(0, True, True)
    lax.fori_loop(1, hops_left, middle, 0)
    step(hops_left, False, False)

    own = term(0)
    sum_left(hops_left - 1).wait_recv()
    own = own + in_left[hops_left - 1].astype(F32)
    sum_right(hops_right - 1).wait_recv()
    own = own + in_right[hops_right - 1].astype(F32)
    sum_ref[...] = own.astype(BF16)
    arrived_left(hops_left - 1).wait_recv()
    arrived_right(hops_right - 1).wait_recv()

    def drain_left(s, carry):
        sum_left(s).wait_send()
        gather_left(s).wait_send()
        return carry

    def drain_right(s, carry):
        sum_right(s).wait_send()
        gather_right(s).wait_send()
        return carry

    lax.fori_loop(0, hops_left, drain_left, 0)
    lax.fori_loop(0, hops_right, drain_right, 0)


def ring(grad_blocks, proj, attended):
    count, tok_rows, depth = grad_blocks.shape
    width = attended.shape[1]
    right = count // 2
    left = count - 1 - right
    vmem = pl.BlockSpec(memory_space=pltpu.VMEM)
    dma = pltpu.SemaphoreType.DMA
    return pl.pallas_call(
        functools.partial(ring_kernel, count),
        out_shape=(
            jax.ShapeDtypeStruct((count, tok_rows, width), BF16),
            jax.ShapeDtypeStruct((tok_rows, width), BF16),
        ),
        in_specs=[vmem] * 3,
        out_specs=(vmem, vmem),
        scratch_shapes=[
            pltpu.VMEM((right, tok_rows, width), BF16),
            pltpu.VMEM((left, tok_rows, width), BF16),
            pltpu.VMEM((right, tok_rows, width), BF16),
            pltpu.VMEM((left, tok_rows, width), BF16),
        ]
        + [dma((right,)), dma((right,)), dma((left,)), dma((left,))] * 2,
        compiler_params=pltpu.CompilerParams(
            collective_id=0, has_side_effects=True, vmem_limit_bytes=48 << 20
        ),
        cost_estimate=pl.CostEstimate(
            flops=2 * count * tok_rows * depth * width,
            bytes_accessed=4 * count * tok_rows * width,
            transcendentals=0,
        ),
    )(grad_blocks, proj, attended)


def shards(queries, rotated_keys, value_vectors, out_grad, out_proj, seg_ids):
    logit_scale = 168.0 ** (-0.5)
    tok_rows, heads_query, head_size = queries.shape
    heads_kv = rotated_keys.shape[1]
    per_kv = heads_query // heads_kv
    ctx_count = lax.axis_size("ctx")
    head_count = lax.axis_size("head")
    ctx_index = lax.axis_index("ctx")
    head_index = lax.axis_index("head")
    group = heads_kv
    groups = [[g * group + i for i in range(group)] for g in range(ctx_count // group)]
    rows = group * tok_rows
    halo_blocks = WINDOW_TOKENS // rows
    q_width = per_kv * head_size

    def to_heads(value):
        return lax.all_to_all(value, "ctx", 1, 0, axis_index_groups=groups, tiled=True)

    def to_tokens(value):
        return lax.all_to_all(value, "ctx", 0, 1, axis_index_groups=groups, tiled=True)

    packed = jnp.concatenate(
        [queries.reshape(tok_rows, heads_kv, q_width), rotated_keys, value_vectors], axis=2
    )
    mine = to_heads(packed).reshape(rows, q_width + 2 * head_size)
    q = mine[:, :q_width].reshape(rows, per_kv, head_size).transpose(1, 0, 2)
    own_kv = mine[:, q_width:]
    received = [shifted(own_kv, "ctx", group * (d + 1)) for d in range(halo_blocks)]
    kv = jnp.concatenate(received[::-1] + [own_kv], axis=0)
    keys, values = kv[:, :head_size], kv[:, head_size:]

    columns = out_grad.shape[1]
    grad_full = jnp.zeros((tok_rows, columns * head_count), BF16)
    grad_full = lax.dynamic_update_slice_in_dim(grad_full, out_grad, head_index * columns, 1)
    for d in range(1, head_count):
        block = rotated(out_grad, "head", d)
        source = lax.rem(head_index + head_count - d, head_count)
        grad_full = lax.dynamic_update_slice_in_dim(grad_full, block, source * columns, 1)
    grad_columns = lax.all_to_all(grad_full, "ctx", 1, 0, tiled=True)

    first_row = (ctx_index // group) * rows
    seg_padded = jnp.concatenate([jnp.full((WINDOW_TOKENS,), -1, jnp.int32), seg_ids], 0)
    key_seg = lax.dynamic_slice_in_dim(seg_padded, first_row, WINDOW_TOKENS + rows, 0)
    query_seg = lax.dynamic_slice_in_dim(seg_ids, first_row, rows, 0)
    query_pos = first_row + jnp.arange(rows, dtype=jnp.int32)
    key_pos = first_row - WINDOW_TOKENS + jnp.arange(WINDOW_TOKENS + rows, dtype=jnp.int32)
    allowed = (key_pos[None, :] <= query_pos[:, None]) & (
        query_pos[:, None] - key_pos[None, :] < WINDOW_TOKENS
    )
    allowed = allowed & (key_pos[None, :] >= 0) & (query_seg[:, None] == key_seg[None, :])

    scores = logit_scale * jnp.einsum("htd,sd->hts", q, keys, preferred_element_type=F32)
    scores = jnp.where(allowed, scores, -1e30)
    top_score = jnp.max(scores, axis=2, keepdims=True)
    weights = jnp.where(allowed, jnp.exp(scores - top_score), 0.0)
    probs = weights / jnp.sum(weights, axis=2, keepdims=True)
    probs_bf = probs.astype(BF16)
    attended = jnp.einsum("hts,sd->htd", probs_bf, values, preferred_element_type=F32).astype(BF16)
    attended_tok = to_tokens(attended.transpose(1, 0, 2).reshape(rows, q_width))

    proj_rows = out_proj.shape[0]
    pad = -proj_rows % 128
    grad_blocks = grad_columns.reshape(ctx_count, tok_rows, proj_rows)
    attended_all, grad_att_tok = ring(
        jnp.pad(grad_blocks, ((0, 0), (0, 0), (0, pad))),
        jnp.pad(out_proj, ((0, pad), (0, 0))),
        attended_tok,
    )
    attended_all = attended_all.reshape(ctx_count * tok_rows, heads_query * head_size)
    grad_att = to_heads(grad_att_tok).reshape(rows, per_kv, head_size).transpose(1, 0, 2)

    out_part = matmul(attended_all, out_proj, ((1,), (1,))).astype(BF16)
    out_part = lax.all_to_all(out_part, "ctx", 0, 1, tiled=True)
    layer_out = lax.dynamic_slice_in_dim(out_part, head_index * columns, columns, 1).astype(F32)
    for d in range(1, head_count):
        target = lax.rem(head_index + d, head_count)
        block = lax.dynamic_slice_in_dim(out_part, target * columns, columns, 1)
        layer_out = layer_out + rotated(block, "head", d).astype(F32)
    layer_out = layer_out.astype(BF16)

    grad_proj = matmul(grad_columns, attended_all, ((0,), (0,))) * (ctx_count * tok_rows) ** (-0.5)

    grad_probs = jnp.einsum("htd,sd->hts", grad_att, values, preferred_element_type=F32)
    row_delta = jnp.sum(grad_att.astype(F32) * attended.astype(F32), axis=2, keepdims=True)
    grad_scores = (probs * (grad_probs - row_delta)).astype(BF16)
    grad_k = logit_scale * jnp.einsum("hts,htd->sd", grad_scores, q, preferred_element_type=F32)
    grad_v = jnp.einsum("hts,htd->sd", probs_bf, grad_att, preferred_element_type=F32)
    grad_kv = jnp.concatenate([grad_k, grad_v], axis=1)
    own_grad = grad_kv[WINDOW_TOKENS:]
    for d in range(1, halo_blocks + 1):
        start = WINDOW_TOKENS - d * rows
        own_grad = own_grad + shifted(
            grad_kv[start : start + rows].astype(BF16), "ctx", -group * d
        ).astype(F32)
    grad_q = logit_scale * jnp.einsum("hts,sd->thd", grad_scores, keys, preferred_element_type=F32)
    grads = jnp.concatenate([grad_q.astype(BF16).reshape(rows, q_width), own_grad.astype(BF16)], 1)
    grads = to_tokens(grads).reshape(tok_rows, heads_kv, q_width + 2 * head_size)
    query_gradient = grads[:, :, :q_width].reshape(tok_rows, heads_query, head_size)
    grad_key = grads[:, :, q_width : q_width + head_size]
    grad_value = grads[:, :, q_width + head_size :]
    return (layer_out, query_gradient, grad_key, grad_value, grad_proj)


def solution(mesh):
    tokens_heads = P("ctx", "head", None)
    both = P("ctx", "head")
    return jax.shard_map(
        shards,
        mesh=mesh,
        in_specs=(tokens_heads, tokens_heads, tokens_heads, both, both, P()),
        out_specs=(both, tokens_heads, tokens_heads, tokens_heads, both),
        check_vma=False,
    )
```

```python
import functools

import jax
import jax.numpy as jnp
from jax import lax
from jax.experimental import pallas as pl
from jax.experimental.pallas import tpu as pltpu
from jax.sharding import PartitionSpec as P

WINDOW_TOKENS = 1024
BF16 = jnp.bfloat16
F32 = jnp.float32


def shifted(value, axis, by):
    count = lax.axis_size(axis)
    pairs = [(i, i + by) for i in range(count) if 0 <= i + by < count]
    return lax.ppermute(value, axis, pairs)


def rotated(value, axis, by):
    count = lax.axis_size(axis)
    return lax.ppermute(value, axis, [(i, (i + by) % count) for i in range(count)])


def matmul(a, b, dims):
    return lax.dot_general(a, b, (dims, ((), ())), preferred_element_type=F32)


def ring_place(position, count):
    half = count // 2
    down = position // half
    step = lax.rem(position, half)
    pair, core = step // 2, lax.rem(step, 2)
    level = pair + down * (half // 2 - 1 - 2 * pair)
    return level * 4 + down * 2 + core


def ring_position(index, count):
    half = count // 2
    level, down, core = index // 4, lax.rem(index // 2, 2), lax.rem(index, 2)
    pair = level + down * (half // 2 - 1 - 2 * level)
    return down * half + pair * 2 + core


def neighbours(count):
    here = ring_position(lax.axis_index("ctx"), count)

    def place(offset):
        return ring_place(lax.rem(here + offset + count, count), count)

    right, left = {"ctx": place(1)}, {"ctx": place(-1)}
    barrier = pltpu.get_barrier_semaphore()
    for neighbour in (left, right):
        pl.semaphore_signal(
            barrier, inc=1, device_id=neighbour, device_id_type=pl.DeviceIdType.MESH
        )
    pl.semaphore_wait(barrier, 2)
    return place, right, left


def remote(src, dst, sems, s, target):
    send, recv = sems
    return pltpu.make_async_remote_copy(
        src_ref=src,
        dst_ref=dst,
        send_sem=send.at[s],
        recv_sem=recv.at[s],
        device_id=target,
        device_id_type=pl.DeviceIdType.MESH,
    )


def gather_kernel(count, own_ref, all_ref, r_send, r_recv, l_send, l_recv):
    hops_right = count // 2
    hops_left = count - 1 - hops_right
    place, right, left = neighbours(count)

    def block_right(s, sem):
        slot = all_ref.at[place(-s)]
        return remote(slot, slot, (r_send, r_recv), sem, right)

    def block_left(s, sem):
        slot = all_ref.at[place(s)]
        return remote(slot, slot, (l_send, l_recv), sem, left)

    all_ref[lax.axis_index("ctx")] = own_ref[...]
    block_right(0, 0).start()
    block_left(0, 0).start()

    def middle(s, carry):
        block_right(s, s - 1).wait_recv()
        block_right(s, s).start()
        block_left(s, s - 1).wait_recv()
        block_left(s, s).start()
        return carry

    lax.fori_loop(1, hops_left, middle, 0)
    block_right(hops_left, hops_left - 1).wait_recv()
    block_right(hops_left, hops_left).start()
    block_left(hops_left, hops_left - 1).wait_recv()
    block_right(hops_right, hops_right - 1).wait_recv()

    def drain_left(s, carry):
        block_left(s, s).wait_send()
        return carry

    def drain_right(s, carry):
        block_right(s, s).wait_send()
        return carry

    lax.fori_loop(0, hops_left, drain_left, 0)
    lax.fori_loop(0, hops_right, drain_right, 0)


def sum_kernel(
    count,
    grad_ref,
    proj_ref,
    sum_ref,
    out_right,
    out_left,
    in_right,
    in_left,
    r_send,
    r_recv,
    l_send,
    l_recv,
):
    hops_right = count // 2
    hops_left = count - 1 - hops_right
    group = proj_ref.shape[0]
    place, right, left = neighbours(count)

    def sum_right(s):
        return remote(out_right.at[s], in_right.at[s], (r_send, r_recv), s, right)

    def sum_left(s):
        return remote(out_left.at[s], in_left.at[s], (l_send, l_recv), s, left)

    def term(offset):
        owner = place(offset)
        return jnp.dot(
            grad_ref[owner // group], proj_ref[lax.rem(owner, group)], preferred_element_type=F32
        )

    def step(s, first, both):
        own = term(hops_right - s)
        if not first:
            sum_right(s - 1).wait_recv()
            own = own + in_right[s - 1].astype(F32)
        out_right[s] = own.astype(BF16)
        sum_right(s).start()
        if both:
            own = term(s - hops_left)
            if not first:
                sum_left(s - 1).wait_recv()
                own = own + in_left[s - 1].astype(F32)
            out_left[s] = own.astype(BF16)
            sum_left(s).start()

    def middle(s, carry):
        step(s, False, True)
        return carry

    step(0, True, True)
    lax.fori_loop(1, hops_left, middle, 0)
    step(hops_left, False, False)

    own = term(0)
    sum_left(hops_left - 1).wait_recv()
    own = own + in_left[hops_left - 1].astype(F32)
    sum_right(hops_right - 1).wait_recv()
    own = own + in_right[hops_right - 1].astype(F32)
    sum_ref[...] = own.astype(BF16)

    def drain_left(s, carry):
        sum_left(s).wait_send()
        return carry

    def drain_right(s, carry):
        sum_right(s).wait_send()
        return carry

    lax.fori_loop(0, hops_left, drain_left, 0)
    lax.fori_loop(0, hops_right, drain_right, 0)


def ring_call(kernel, number, operands, result, scratch, count, flops):
    right = count // 2
    left = count - 1 - right
    dma = pltpu.SemaphoreType.DMA
    vmem = pl.BlockSpec(memory_space=pltpu.VMEM)
    return pl.pallas_call(
        functools.partial(kernel, count),
        out_shape=jax.ShapeDtypeStruct(result, BF16),
        in_specs=[vmem] * len(operands),
        out_specs=vmem,
        scratch_shapes=scratch + [dma((right,)), dma((right,)), dma((left,)), dma((left,))],
        compiler_params=pltpu.CompilerParams(
            collective_id=number, has_side_effects=True, vmem_limit_bytes=48 << 20
        ),
        cost_estimate=pl.CostEstimate(
            flops=flops, bytes_accessed=64 << 20, transcendentals=0
        ),
    )(*operands)


def ring_gather(block, count):
    return ring_call(gather_kernel, 0, (block,), (count,) + block.shape, [], count, 0)


def ring_sum(grad_groups, proj_heads, count):
    rows, depth = grad_groups.shape[1:]
    width = proj_heads.shape[2]
    right = count // 2
    left = count - 1 - right
    scratch = [pltpu.VMEM((hops, rows, width), BF16) for hops in (right, left, right, left)]
    flops = 2 * count * rows * depth * width
    return ring_call(
        sum_kernel, 1, (grad_groups, proj_heads), (rows, width), scratch, count, flops
    )


def shards(queries, rotated_keys, value_vectors, out_grad, out_proj, seg_ids):
    logit_scale = 168.0 ** (-0.5)
    tok_rows, heads_query, head_size = queries.shape
    heads_kv = rotated_keys.shape[1]
    per_kv = heads_query // heads_kv
    ctx_count = lax.axis_size("ctx")
    head_count = lax.axis_size("head")
    ctx_index = lax.axis_index("ctx")
    head_index = lax.axis_index("head")
    group = heads_kv
    groups = [[g * group + i for i in range(group)] for g in range(ctx_count // group)]
    rows = group * tok_rows
    halo_blocks = WINDOW_TOKENS // rows
    q_width = per_kv * head_size

    def to_heads(value):
        return lax.all_to_all(value, "ctx", 1, 0, axis_index_groups=groups, tiled=True)

    def to_tokens(value):
        return lax.all_to_all(value, "ctx", 0, 1, axis_index_groups=groups, tiled=True)

    packed = jnp.concatenate(
        [queries.reshape(tok_rows, heads_kv, q_width), rotated_keys, value_vectors], axis=2
    )
    mine = to_heads(packed).reshape(rows, q_width + 2 * head_size)
    q = mine[:, :q_width].reshape(rows, per_kv, head_size).transpose(1, 0, 2)
    own_kv = mine[:, q_width:]
    received = [shifted(own_kv, "ctx", group * (d + 1)) for d in range(halo_blocks)]
    kv = jnp.concatenate(received[::-1] + [own_kv], axis=0)
    columns = out_grad.shape[1]
    grad_full = jnp.zeros((tok_rows, columns * head_count), BF16)
    grad_full = lax.dynamic_update_slice_in_dim(grad_full, out_grad, head_index * columns, 1)
    for d in range(1, head_count):
        block = rotated(out_grad, "head", d)
        source = lax.rem(head_index + head_count - d, head_count)
        grad_full = lax.dynamic_update_slice_in_dim(grad_full, block, source * columns, 1)
    grad_full, kv = lax.optimization_barrier((grad_full, kv))
    keys, values = kv[:, :head_size], kv[:, head_size:]
    grad_columns = lax.all_to_all(grad_full, "ctx", 1, 0, tiled=True)

    first_row = (ctx_index // group) * rows
    seg_padded = jnp.concatenate([jnp.full((WINDOW_TOKENS,), -1, jnp.int32), seg_ids], 0)
    key_seg = lax.dynamic_slice_in_dim(seg_padded, first_row, WINDOW_TOKENS + rows, 0)
    query_seg = lax.dynamic_slice_in_dim(seg_ids, first_row, rows, 0)
    query_pos = first_row + jnp.arange(rows, dtype=jnp.int32)
    key_pos = first_row - WINDOW_TOKENS + jnp.arange(WINDOW_TOKENS + rows, dtype=jnp.int32)
    allowed = (key_pos[None, :] <= query_pos[:, None]) & (
        query_pos[:, None] - key_pos[None, :] < WINDOW_TOKENS
    )
    allowed = allowed & (key_pos[None, :] >= 0) & (query_seg[:, None] == key_seg[None, :])

    scores = logit_scale * jnp.einsum("htd,sd->hts", q, keys, preferred_element_type=F32)
    scores = jnp.where(allowed, scores, -1e30)
    top_score = jnp.max(scores, axis=2, keepdims=True)
    weights = jnp.where(allowed, jnp.exp(scores - top_score), 0.0)
    probs = weights / jnp.sum(weights, axis=2, keepdims=True)
    probs_bf = probs.astype(BF16)
    attended = jnp.einsum("hts,sd->htd", probs_bf, values, preferred_element_type=F32).astype(BF16)

    attended_all = ring_gather(attended.transpose(1, 0, 2).reshape(rows, q_width), ctx_count)
    attended_all = attended_all.reshape(ctx_count // group, group, rows, q_width)
    attended_all = attended_all.transpose(0, 2, 1, 3).reshape(ctx_count * tok_rows, group * q_width)
    out_part = matmul(attended_all, out_proj, ((1,), (1,))).astype(BF16)
    out_part, grad_columns = lax.optimization_barrier((out_part, grad_columns))
    out_part = lax.all_to_all(out_part, "ctx", 0, 1, tiled=True)
    layer_out = lax.dynamic_slice_in_dim(out_part, head_index * columns, columns, 1).astype(F32)
    for d in range(1, head_count):
        target = lax.rem(head_index + d, head_count)
        block = lax.dynamic_slice_in_dim(out_part, target * columns, columns, 1)
        layer_out = layer_out + rotated(block, "head", d).astype(F32)
    layer_out = layer_out.astype(BF16)

    grad_proj = matmul(grad_columns, attended_all, ((0,), (0,))) * (ctx_count * tok_rows) ** (-0.5)

    proj_rows = out_proj.shape[0]
    pad = -proj_rows % 128
    proj_heads = out_proj.reshape(proj_rows, group, q_width).transpose(1, 0, 2)
    grad_att = ring_sum(
        jnp.pad(grad_columns.reshape(-1, rows, proj_rows), ((0, 0), (0, 0), (0, pad))),
        jnp.pad(proj_heads, ((0, 0), (0, pad), (0, 0))),
        ctx_count,
    )
    grad_att = grad_att.reshape(rows, per_kv, head_size).transpose(1, 0, 2)

    grad_probs = jnp.einsum("htd,sd->hts", grad_att, values, preferred_element_type=F32)
    row_delta = jnp.sum(grad_att.astype(F32) * attended.astype(F32), axis=2, keepdims=True)
    grad_scores = (probs * (grad_probs - row_delta)).astype(BF16)
    grad_k = logit_scale * jnp.einsum("hts,htd->sd", grad_scores, q, preferred_element_type=F32)
    grad_v = jnp.einsum("hts,htd->sd", probs_bf, grad_att, preferred_element_type=F32)
    grad_kv = jnp.concatenate([grad_k, grad_v], axis=1)
    own_grad = grad_kv[WINDOW_TOKENS:]
    for d in range(1, halo_blocks + 1):
        start = WINDOW_TOKENS - d * rows
        own_grad = own_grad + shifted(
            grad_kv[start : start + rows].astype(BF16), "ctx", -group * d
        ).astype(F32)
    grad_q = logit_scale * jnp.einsum("hts,sd->thd", grad_scores, keys, preferred_element_type=F32)
    grads = jnp.concatenate([grad_q.astype(BF16).reshape(rows, q_width), own_grad.astype(BF16)], 1)
    grads = to_tokens(grads).reshape(tok_rows, heads_kv, q_width + 2 * head_size)
    query_gradient = grads[:, :, :q_width].reshape(tok_rows, heads_query, head_size)
    grad_key = grads[:, :, q_width : q_width + head_size]
    grad_value = grads[:, :, q_width + head_size :]
    return (layer_out, query_gradient, grad_key, grad_value, grad_proj)


def solution(mesh):
    tokens_heads = P("ctx", "head", None)
    both = P("ctx", "head")
    return jax.shard_map(
        shards,
        mesh=mesh,
        in_specs=(tokens_heads, tokens_heads, tokens_heads, both, both, P()),
        out_specs=(both, tokens_heads, tokens_heads, tokens_heads, both),
        check_vma=False,
    )
```

```python
import functools

import jax
import jax.numpy as jnp
from jax import lax
from jax.experimental import pallas as pl
from jax.experimental.pallas import tpu as pltpu
from jax.sharding import PartitionSpec as P

WINDOW_TOKENS = 1024
BF16 = jnp.bfloat16
F32 = jnp.float32


def shifted(value, axis, by):
    count = lax.axis_size(axis)
    pairs = [(i, i + by) for i in range(count) if 0 <= i + by < count]
    return lax.ppermute(value, axis, pairs)


def rotated(value, axis, by):
    count = lax.axis_size(axis)
    return lax.ppermute(value, axis, [(i, (i + by) % count) for i in range(count)])


def matmul(a, b, dims):
    return lax.dot_general(a, b, (dims, ((), ())), preferred_element_type=F32)


def ring_place(position, count):
    half = count // 2
    down = position // half
    step = lax.rem(position, half)
    pair, core = step // 2, lax.rem(step, 2)
    level = pair + down * (half // 2 - 1 - 2 * pair)
    return level * 4 + down * 2 + core


def ring_position(index, count):
    half = count // 2
    level, down, core = index // 4, lax.rem(index // 2, 2), lax.rem(index, 2)
    pair = level + down * (half // 2 - 1 - 2 * level)
    return down * half + pair * 2 + core


def neighbours(count, everyone=False):
    me = lax.axis_index("ctx")
    here = ring_position(lax.axis_index("ctx"), count)

    def place(offset):
        return ring_place(lax.rem(here + offset + count, count), count)

    right, left = {"ctx": place(1)}, {"ctx": place(-1)}
    barrier = pltpu.get_barrier_semaphore()
    others = (left, right)
    if everyone:
        others = [{"ctx": lax.rem(me + d, count)} for d in range(1, count)]
    for other in others:
        pl.semaphore_signal(barrier, inc=1, device_id=other, device_id_type=pl.DeviceIdType.MESH)
    pl.semaphore_wait(barrier, len(others))
    return place, right, left


def remote(src, dst, sems, s, target):
    send, recv = sems
    return pltpu.make_async_remote_copy(
        src_ref=src,
        dst_ref=dst,
        send_sem=send.at[s],
        recv_sem=recv.at[s],
        device_id=target,
        device_id_type=pl.DeviceIdType.MESH,
    )


def gather_kernel(count, own_ref, all_ref, r_send, r_recv, l_send, l_recv):
    hops_right = count // 2
    hops_left = count - 1 - hops_right
    place, right, left = neighbours(count)

    def block_right(s, sem):
        slot = all_ref.at[place(-s)]
        return remote(slot, slot, (r_send, r_recv), sem, right)

    def block_left(s, sem):
        slot = all_ref.at[place(s)]
        return remote(slot, slot, (l_send, l_recv), sem, left)

    all_ref[lax.axis_index("ctx")] = own_ref[...]
    block_right(0, 0).start()
    block_left(0, 0).start()

    def middle(s, carry):
        block_right(s, s - 1).wait_recv()
        block_right(s, s).start()
        block_left(s, s - 1).wait_recv()
        block_left(s, s).start()
        return carry

    lax.fori_loop(1, hops_left, middle, 0)
    block_right(hops_left, hops_left - 1).wait_recv()
    block_right(hops_left, hops_left).start()
    block_left(hops_left, hops_left - 1).wait_recv()
    block_right(hops_right, hops_right - 1).wait_recv()

    def drain_left(s, carry):
        block_left(s, s).wait_send()
        return carry

    def drain_right(s, carry):
        block_right(s, s).wait_send()
        return carry

    lax.fori_loop(0, hops_left, drain_left, 0)
    lax.fori_loop(0, hops_right, drain_right, 0)


def sum_kernel(
    count,
    grad_ref,
    proj_ref,
    part_ref,
    sum_ref,
    blocks_ref,
    out_right,
    out_left,
    in_right,
    in_left,
    b_send,
    b_recv,
    r_send,
    r_recv,
    l_send,
    l_recv,
):
    me = lax.axis_index("ctx")
    hops_right = count // 2
    hops_left = count - 1 - hops_right
    group = proj_ref.shape[0]
    place, right, left = neighbours(count, everyone=True)

    def block_out(d):
        target = lax.rem(me + d, count)
        return remote(
            part_ref.at[target], blocks_ref.at[me], (b_send, b_recv), d - 1, {"ctx": target}
        )

    def block_in(d):
        source = lax.rem(me - d + count, count)
        return remote(
            part_ref.at[source], blocks_ref.at[source], (b_send, b_recv), d - 1, {"ctx": source}
        )

    blocks_ref[me] = part_ref[me]

    def sum_right(s):
        return remote(out_right.at[s], in_right.at[s], (r_send, r_recv), s, right)

    def sum_left(s):
        return remote(out_left.at[s], in_left.at[s], (l_send, l_recv), s, left)

    def term(offset):
        owner = place(offset)
        return jnp.dot(
            grad_ref[owner // group], proj_ref[lax.rem(owner, group)], preferred_element_type=F32
        )

    def step(s, first, both):
        own = term(hops_right - s)
        if not first:
            sum_right(s - 1).wait_recv()
            own = own + in_right[s - 1].astype(F32)
        out_right[s] = own.astype(BF16)
        sum_right(s).start()
        block_out(2 * s + 1).start()
        if both:
            own = term(s - hops_left)
            if not first:
                sum_left(s - 1).wait_recv()
                own = own + in_left[s - 1].astype(F32)
            out_left[s] = own.astype(BF16)
            sum_left(s).start()
            block_out(2 * s + 2).start()

    def middle(s, carry):
        step(s, False, True)
        return carry

    step(0, True, True)
    lax.fori_loop(1, hops_left, middle, 0)
    step(hops_left, False, False)

    own = term(0)
    sum_left(hops_left - 1).wait_recv()
    own = own + in_left[hops_left - 1].astype(F32)
    sum_right(hops_right - 1).wait_recv()
    own = own + in_right[hops_right - 1].astype(F32)
    sum_ref[...] = own.astype(BF16)

    def take_blocks(d, carry):
        block_in(d).wait_recv()
        block_out(d).wait_send()
        return carry

    lax.fori_loop(1, count, take_blocks, 0)

    def drain_left(s, carry):
        sum_left(s).wait_send()
        return carry

    def drain_right(s, carry):
        sum_right(s).wait_send()
        return carry

    lax.fori_loop(0, hops_left, drain_left, 0)
    lax.fori_loop(0, hops_right, drain_right, 0)


def ring_call(kernel, number, operands, results, scratch, count, flops):
    right = count // 2
    left = count - 1 - right
    dma = pltpu.SemaphoreType.DMA
    vmem = pl.BlockSpec(memory_space=pltpu.VMEM)
    return pl.pallas_call(
        functools.partial(kernel, count),
        out_shape=[jax.ShapeDtypeStruct(shape, BF16) for shape in results],
        in_specs=[vmem] * len(operands),
        out_specs=[vmem] * len(results),
        scratch_shapes=scratch + [dma((right,)), dma((right,)), dma((left,)), dma((left,))],
        compiler_params=pltpu.CompilerParams(
            collective_id=number, has_side_effects=True, vmem_limit_bytes=48 << 20
        ),
        cost_estimate=pl.CostEstimate(
            flops=flops, bytes_accessed=64 << 20, transcendentals=0
        ),
    )(*operands)


def ring_gather(block, count):
    return ring_call(gather_kernel, 0, (block,), [(count,) + block.shape], [], count, 0)[0]


def ring_sum(grad_groups, proj_heads, parts, count):
    rows, depth = grad_groups.shape[1:]
    width = proj_heads.shape[2]
    right = count // 2
    left = count - 1 - right
    scratch = [pltpu.VMEM((hops, rows, width), BF16) for hops in (right, left, right, left)]
    scratch = scratch + [pltpu.SemaphoreType.DMA((count - 1,))] * 2
    flops = 2 * count * rows * depth * width
    return ring_call(
        sum_kernel,
        1,
        (grad_groups, proj_heads, parts),
        [(rows, width), parts.shape],
        scratch,
        count,
        flops,
    )


def shards(queries, rotated_keys, value_vectors, out_grad, out_proj, seg_ids):
    logit_scale = 168.0 ** (-0.5)
    tok_rows, heads_query, head_size = queries.shape
    heads_kv = rotated_keys.shape[1]
    per_kv = heads_query // heads_kv
    ctx_count = lax.axis_size("ctx")
    head_count = lax.axis_size("head")
    ctx_index = lax.axis_index("ctx")
    head_index = lax.axis_index("head")
    group = heads_kv
    groups = [[g * group + i for i in range(group)] for g in range(ctx_count // group)]
    rows = group * tok_rows
    halo_blocks = WINDOW_TOKENS // rows
    q_width = per_kv * head_size

    def to_heads(value):
        return lax.all_to_all(value, "ctx", 1, 0, axis_index_groups=groups, tiled=True)

    def to_tokens(value):
        return lax.all_to_all(value, "ctx", 0, 1, axis_index_groups=groups, tiled=True)

    packed = jnp.concatenate(
        [queries.reshape(tok_rows, heads_kv, q_width), rotated_keys, value_vectors], axis=2
    )
    mine = to_heads(packed).reshape(rows, q_width + 2 * head_size)
    q = mine[:, :q_width].reshape(rows, per_kv, head_size).transpose(1, 0, 2)
    own_kv = mine[:, q_width:]
    received = [shifted(own_kv, "ctx", group * (d + 1)) for d in range(halo_blocks)]
    kv = jnp.concatenate(received[::-1] + [own_kv], axis=0)
    columns = out_grad.shape[1]
    grad_full = jnp.zeros((tok_rows, columns * head_count), BF16)
    grad_full = lax.dynamic_update_slice_in_dim(grad_full, out_grad, head_index * columns, 1)
    for d in range(1, head_count):
        block = rotated(out_grad, "head", d)
        source = lax.rem(head_index + head_count - d, head_count)
        grad_full = lax.dynamic_update_slice_in_dim(grad_full, block, source * columns, 1)
    grad_full, kv = lax.optimization_barrier((grad_full, kv))
    keys, values = kv[:, :head_size], kv[:, head_size:]
    grad_columns = lax.all_to_all(grad_full, "ctx", 1, 0, tiled=True)

    first_row = (ctx_index // group) * rows
    seg_padded = jnp.concatenate([jnp.full((WINDOW_TOKENS,), -1, jnp.int32), seg_ids], 0)
    key_seg = lax.dynamic_slice_in_dim(seg_padded, first_row, WINDOW_TOKENS + rows, 0)
    query_seg = lax.dynamic_slice_in_dim(seg_ids, first_row, rows, 0)
    query_pos = first_row + jnp.arange(rows, dtype=jnp.int32)
    key_pos = first_row - WINDOW_TOKENS + jnp.arange(WINDOW_TOKENS + rows, dtype=jnp.int32)
    allowed = (key_pos[None, :] <= query_pos[:, None]) & (
        query_pos[:, None] - key_pos[None, :] < WINDOW_TOKENS
    )
    allowed = allowed & (key_pos[None, :] >= 0) & (query_seg[:, None] == key_seg[None, :])

    scores = logit_scale * jnp.einsum("htd,sd->hts", q, keys, preferred_element_type=F32)
    scores = jnp.where(allowed, scores, -1e30)
    top_score = jnp.max(scores, axis=2, keepdims=True)
    weights = jnp.where(allowed, jnp.exp(scores - top_score), 0.0)
    probs = weights / jnp.sum(weights, axis=2, keepdims=True)
    probs_bf = probs.astype(BF16)
    attended = jnp.einsum("hts,sd->htd", probs_bf, values, preferred_element_type=F32).astype(BF16)

    attended_all = ring_gather(attended.transpose(1, 0, 2).reshape(rows, q_width), ctx_count)
    attended_all = attended_all.reshape(ctx_count // group, group, rows, q_width)
    attended_all = attended_all.transpose(0, 2, 1, 3).reshape(ctx_count * tok_rows, group * q_width)
    out_part = matmul(attended_all, out_proj, ((1,), (1,))).astype(BF16)
    grad_proj = matmul(grad_columns, attended_all, ((0,), (0,))) * (ctx_count * tok_rows) ** (-0.5)

    proj_rows = out_proj.shape[0]
    pad = -proj_rows % 128
    proj_heads = out_proj.reshape(proj_rows, group, q_width).transpose(1, 0, 2)
    grad_att, blocks = ring_sum(
        jnp.pad(grad_columns.reshape(-1, rows, proj_rows), ((0, 0), (0, 0), (0, pad))),
        jnp.pad(proj_heads, ((0, 0), (0, pad), (0, 0))),
        out_part.reshape(ctx_count, tok_rows, proj_rows),
        ctx_count,
    )
    per_head = ctx_count // head_count
    layer_out = lax.dynamic_slice_in_dim(blocks, head_index * per_head, per_head, 0).astype(F32)
    for d in range(1, head_count):
        target = lax.rem(head_index + d, head_count)
        block = lax.dynamic_slice_in_dim(blocks, target * per_head, per_head, 0)
        layer_out = layer_out + rotated(block, "head", d).astype(F32)
    layer_out = layer_out.astype(BF16).transpose(1, 0, 2).reshape(tok_rows, columns)
    grad_att = grad_att.reshape(rows, per_kv, head_size).transpose(1, 0, 2)

    grad_probs = jnp.einsum("htd,sd->hts", grad_att, values, preferred_element_type=F32)
    row_delta = jnp.sum(grad_att.astype(F32) * attended.astype(F32), axis=2, keepdims=True)
    grad_scores = (probs * (grad_probs - row_delta)).astype(BF16)
    grad_k = logit_scale * jnp.einsum("hts,htd->sd", grad_scores, q, preferred_element_type=F32)
    grad_v = jnp.einsum("hts,htd->sd", probs_bf, grad_att, preferred_element_type=F32)
    grad_kv = jnp.concatenate([grad_k, grad_v], axis=1)
    own_grad = grad_kv[WINDOW_TOKENS:]
    for d in range(1, halo_blocks + 1):
        start = WINDOW_TOKENS - d * rows
        own_grad = own_grad + shifted(
            grad_kv[start : start + rows].astype(BF16), "ctx", -group * d
        ).astype(F32)
    grad_q = logit_scale * jnp.einsum("hts,sd->thd", grad_scores, keys, preferred_element_type=F32)
    grads = jnp.concatenate([grad_q.astype(BF16).reshape(rows, q_width), own_grad.astype(BF16)], 1)
    grads = to_tokens(grads).reshape(tok_rows, heads_kv, q_width + 2 * head_size)
    query_gradient = grads[:, :, :q_width].reshape(tok_rows, heads_query, head_size)
    grad_key = grads[:, :, q_width : q_width + head_size]
    grad_value = grads[:, :, q_width + head_size :]
    return (layer_out, query_gradient, grad_key, grad_value, grad_proj)


def solution(mesh):
    tokens_heads = P("ctx", "head", None)
    both = P("ctx", "head")
    return jax.shard_map(
        shards,
        mesh=mesh,
        in_specs=(tokens_heads, tokens_heads, tokens_heads, both, both, P()),
        out_specs=(both, tokens_heads, tokens_heads, tokens_heads, both),
        check_vma=False,
    )
```
